256 devices in a mesh: store: 32 (over z, y), tp: 8 (over x, core).
Axes of the slice: x: 4, y: 4, z: 8, core: 2. Of those that a mesh axis runs over, the one named last changes fastest.
Arguments:
- query: bfloat16 [2560, 8192], P('store', 'tp')
- new_kv: bfloat16 [2, 2560, 1024], P(None, 'store', 'tp')
- kv_store: bfloat16 [2, 640, 512, 1024], P(None, 'store', None, 'tp'), may hold values from -6 to 6
- passage_ids: int32 [256, 10], P('store'), may hold values from 0 to 639, as said below
- residual_in: bfloat16 [2560, 8192], P('store', 'tp'), may hold values from -3 to 3
- out_weight: bfloat16 [8192, 8192], P('tp', 'store'), may hold values from -0.75 to 0.75
Outputs:
- layer_out: bfloat16 [2560, 8192], P('store', 'tp')
The draws below stay inside these ranges and needn't reach their ends.
Inputs may be any that keep to these rules, and one draw needn't show every extreme that they name: `passage_ids`: store shard s holds passages s * 20 to (s + 1) * 20 - 1. In each aligned block of 8 rows (the queries of one index of store), every shard that is named at all is named exactly 5 times; popular shards are named in more blocks and low passage numbers within a shard are more popular.
All inputs are finite; a program needn't handle non-finite values.
Results may differ from the reference program's by a relative error of at most 0.018.
Values may be sent and summed in bfloat16 or wider, within the bound.
A program may use at most 64 MiB of HBM per device.

```python
import jax
import jax.numpy as jnp
from jax import lax

D = 8192
H = 64
KVH = 8
HD = 128
PLEN = 512
RET = 10
QRY_DEV = 8
PASS_DEV = 20
QUERIES = 256
STREAMS = 2560
PASSAGES = 640
N_TP = 8


def shared_tokens(key):
    base_key = jax.random.fold_in(key, 5151)
    key_one, key_two, key_three = jax.random.split(base_key, 3)
    new_keys = jax.random.normal(key_one, (STREAMS, KVH * HD), jnp.float32)
    new_values = jax.random.normal(key_two, (STREAMS, KVH * HD), jnp.float32)
    queries = jax.random.normal(key_three, (STREAMS, H * HD), jnp.float32)
    return (queries, new_keys, new_values)


def draw_query(key, part):
    queries, new_keys, new_values = shared_tokens(key)
    return queries.astype(jnp.bfloat16)


def draw_new_kv(key, part):
    queries, new_keys, new_values = shared_tokens(key)
    return jnp.stack([new_keys, new_values]).astype(jnp.bfloat16)


def shuffled(one_key):
    return jax.random.permutation(one_key, RET * QRY_DEV)


def draw_passage_ids(key, part):
    shard_count = PASSAGES // PASS_DEV
    fan_out = min(shard_count, 16)
    stream_count = RET * QRY_DEV
    per_shard = stream_count // fan_out
    key_one, key_two, key_three, key_four, key_five = jax.random.split(jax.random.fold_in(key, 9090), 5)
    popularity = jax.random.randint(key_one, (shard_count,), 0, 3) * 3000
    block_noise = jax.random.randint(key_two, (shard_count, shard_count), 0, 4096)
    rank_scores = (block_noise + popularity[None, :]) * shard_count + jnp.arange(shard_count)[None, :]
    picked_scores, chosen_shards = lax.top_k(rank_scores, fan_out)
    orderings = jax.vmap(shuffled)(jax.random.split(key_three, shard_count))
    owners = jnp.take_along_axis(chosen_shards, orderings // per_shard, axis=1)
    first_pick = jax.random.randint(key_four, (shard_count, stream_count), 0, PASS_DEV)
    second_pick = jax.random.randint(key_five, (shard_count, stream_count), 0, PASS_DEV)
    local_index = jnp.minimum(first_pick, second_pick)
    return (owners * PASS_DEV + local_index).reshape(QUERIES, RET).astype(jnp.int32)


def levels(key, shape, cuts, smallest, top_value):
    factor_of = 1.0
    for position, shards_of in cuts:
        steps = jax.random.uniform(jax.random.fold_in(jax.random.fold_in(key, 6), position), (shards_of,), jnp.float32, smallest / len(cuts), top_value / len(cuts))
        factor_of = factor_of * jnp.repeat(jnp.exp(steps), shape[position] // shards_of).reshape((-1,) + (1,) * (len(shape) - 1 - position))
    return factor_of


def bell_draw(own_key, shape, deviation, bound, shards=(), held_as=jnp.bfloat16):
    values = jax.random.normal(own_key, shape, jnp.float32) * deviation
    if len(shards) > 0:
        values = levels(own_key, shape, shards, -0.22, 0.18) * values
    return jnp.clip(values, min=-bound, max=bound).astype(held_as)


def setup_inputs(seed: int = 0) -> dict:
    streams_of = jax.random.split(jax.random.key(seed), 7)
    return {
        "query": draw_query(jax.random.fold_in(streams_of[6], 71), 0),
        "new_kv": draw_new_kv(jax.random.fold_in(streams_of[6], 71), 0),
        "kv_store": bell_draw(streams_of[2], (2, PASSAGES, PLEN, KVH * HD), 1.0, 6.0, ((1, 32), (3, 8))),
        "passage_ids": draw_passage_ids(jax.random.fold_in(streams_of[6], 71), 0),
        "residual_in": bell_draw(streams_of[4], (STREAMS, D), 0.5, 3.0, ((0, 32), (1, 8))),
        "out_weight": bell_draw(streams_of[5], (H * HD, D), 0.125, 0.75, ((0, 8), (1, 32))),
    }


def attend_block(packed, kv_store):
    block_queries, block_keys, block_values, block_ids = packed
    slot_count = block_queries.shape[0]
    group_size = H // KVH
    scaling = 1.0 / (HD ** 0.5)
    stored_keys = kv_store[0][block_ids].astype(jnp.float32).reshape(slot_count, PLEN, KVH, HD)
    stored_values = kv_store[1][block_ids].astype(jnp.float32).reshape(slot_count, PLEN, KVH, HD)
    query_heads = block_queries.astype(jnp.float32).reshape(slot_count, KVH, group_size, HD)
    own_keys = block_keys.astype(jnp.float32).reshape(slot_count, KVH, HD)
    own_values = block_values.astype(jnp.float32).reshape(slot_count, KVH, HD)
    scores = jnp.einsum("bgjd,bkgd->bgjk", query_heads, stored_keys) * scaling
    own_score = jnp.einsum("bgjd,bgd->bgj", query_heads, own_keys) * scaling
    highest = jnp.maximum(jnp.max(scores, axis=-1), own_score)
    exponent_terms = jnp.exp(scores - highest[..., None])
    own_term = jnp.exp(own_score - highest)
    totals = jnp.sum(exponent_terms, axis=-1) + own_term
    weights = (exponent_terms / totals[..., None]).astype(jnp.bfloat16)
    own_weight = (own_term / totals).astype(jnp.bfloat16)
    mixed = jnp.einsum("bgjk,bkgd->bgjd", weights.astype(jnp.float32), stored_values)
    mixed = mixed + own_weight.astype(jnp.float32)[..., None] * own_values[:, :, None, :]
    return mixed.astype(jnp.bfloat16).reshape(slot_count, H * HD)


def reference(query, new_kv, kv_store, passage_ids, residual_in, out_weight):
    flat_ids = passage_ids.reshape(STREAMS).astype(jnp.int32)
    block_count = STREAMS // RET
    packed = (query.reshape(block_count, RET, H * HD),
              new_kv[0].reshape(block_count, RET, KVH * HD),
              new_kv[1].reshape(block_count, RET, KVH * HD),
              flat_ids.reshape(block_count, RET))
    attention = lax.map(lambda piece: attend_block(piece, kv_store), packed)
    attention = attention.reshape(STREAMS, H * HD)
    group_width = H * HD // N_TP
    projected = jnp.zeros((STREAMS, D), jnp.float32)
    for group in range(N_TP):
        part_rows = attention[:, group * group_width:(group + 1) * group_width]
        part_weight = out_weight[group * group_width:(group + 1) * group_width, :]
        partial_sum = jnp.dot(part_rows, part_weight, preferred_element_type=jnp.float32)
        projected = projected + partial_sum.astype(jnp.bfloat16).astype(jnp.float32)
    return (residual_in.astype(jnp.float32) + projected).astype(jnp.bfloat16)
```

```python
import functools

import jax
import jax.numpy as jnp
import numpy as np
from jax import lax
from jax.experimental import pallas as pl
from jax.experimental.pallas import tpu as pltpu
from jax.sharding import PartitionSpec as P

HD = 128
PLEN = 512
GROUP = 8
SLOTS = 5
BLOCK = 16
WIDE = 3 * HD
PAD = 128
CHUNK = 16
Y_CHIPS = 4
MESH = pl.DeviceIdType.MESH
BF = jnp.bfloat16
F32 = jnp.float32
SCALE = 1.0 / HD**0.5
VMEM = pl.BlockSpec(memory_space=pltpu.VMEM)


def iota(shape, dim):
    return lax.broadcasted_iota(jnp.int32, shape, dim)


def dot(a, b):
    return jnp.dot(a, b, preferred_element_type=F32)


def row_parts(k):
    inner = jnp.bitwise_and(k, BLOCK - 1)
    group = (
        (inner >= SLOTS).astype(jnp.int32)
        + (inner >= 2 * SLOTS).astype(jnp.int32)
        + (inner >= 3 * SLOTS).astype(jnp.int32)
    )
    slot = jnp.right_shift(k, 4) * SLOTS + inner - SLOTS * group
    return slot, group


def as_row(column):
    return jnp.transpose(jnp.broadcast_to(column, (column.shape[0], HD)))[0:1, :]


def stream_slots(ids, pass_local):
    rows, width = ids.shape
    stream = iota((PAD, width), 0)
    spread = jnp.zeros((PAD, width), F32)
    place = jnp.full((PAD, width), -1, jnp.int32)
    for r in range(rows):
        inside = (stream >= r * width) & (stream < (r + 1) * width)
        spread = jnp.where(inside, ids[r : r + 1, :].astype(F32), spread)
        place = jnp.where(inside, stream - r * width, place)
    hit = place == iota((PAD, width), 1)
    passage = jnp.sum(jnp.where(hit, spread, 0.0), axis=1, keepdims=True)
    real = iota((PAD, 1), 0) < rows * width
    owner = jnp.floor((passage + 0.5) * (1.0 / pass_local))
    local = jnp.where(real, passage - owner * pass_local, 0.0)
    owner = jnp.where(real, owner, -1.0)
    same = owner == as_row(owner)
    earlier = iota((PAD, PAD), 1) < iota((PAD, PAD), 0)
    position = jnp.sum(jnp.where(same & earlier, 1.0, 0.0), axis=1, keepdims=True)
    return jnp.where(real, owner * SLOTS + position, -1.0), local


def remote(src, dst, send, recv, device):
    return pltpu.make_async_remote_copy(
        src_ref=src, dst_ref=dst, send_sem=send, recv_sem=recv, device_id=device, device_id_type=MESH
    )


def exchange_copy(k, me, tp, stores, msg, recv, send_sem, recv_sem):
    to = lax.rem(me + k, stores)
    return remote(
        msg.at[pl.ds(pl.multiple_of(to * BLOCK, BLOCK), BLOCK)],
        recv.at[pl.ds(pl.multiple_of(me * BLOCK, BLOCK), BLOCK)],
        send_sem.at[k],
        recv_sem.at[k],
        (to, tp),
    )


def route_kernel(stores, pass_local, q_ref, id_ref, recv_ref, wide_ref, msg_ref, send_sem, recv_sem):
    me, tp = lax.axis_index("store"), lax.axis_index("tp")
    barrier = pltpu.get_barrier_semaphore()

    def greet(k, carry):
        pl.semaphore_signal(
            barrier, inc=1, device_id=(lax.rem(me + k, stores), tp), device_id_type=MESH
        )
        return carry

    lax.fori_loop(1, stores, greet, 0)
    streams, width = q_ref.shape
    slot, local = stream_slots(id_ref[...], pass_local)
    wide_ref[...] = jnp.zeros(wide_ref.shape, BF)
    wide_ref[0:streams, 0:width] = q_ref[...]
    wide_ref[:, width:] = jnp.broadcast_to(local, (PAD, HD)).astype(BF)
    rows = stores * BLOCK
    row_slot, row_group = row_parts(iota((rows, 1), 0))
    wanted = jnp.where(row_group < 3, row_slot, -2).astype(F32)
    pick = jnp.where(wanted == as_row(slot), 1.0, 0.0).astype(BF)
    message = dot(pick, wide_ref[:, 2 * WIDE : 3 * WIDE])
    message = jnp.where(row_group == 1, dot(pick, wide_ref[:, WIDE : 2 * WIDE]), message)
    message = jnp.where(row_group == 0, dot(pick, wide_ref[:, 0:WIDE]), message)
    msg_ref[...] = message.astype(BF)
    pl.semaphore_wait(barrier, stores - 1)

    def start(k, carry):
        exchange_copy(k, me, tp, stores, msg_ref, recv_ref, send_sem, recv_sem).start()
        return carry

    lax.fori_loop(1, stores, start, 0)
    mine = pl.ds(pl.multiple_of(me * BLOCK, BLOCK), BLOCK)
    recv_ref[mine, :] = msg_ref[mine, :]

    def finish(k, carry):
        exchange_copy(k, me, tp, stores, msg_ref, recv_ref, send_sem, recv_sem).wait()
        return carry

    lax.fori_loop(1, stores, finish, 0)


def attend_kernel(n_chunks, recv_ref, kv_ref, back_ref, sorted_ref, result_ref):
    rows = recv_ref.shape[0]
    places = sorted_ref.shape[0]
    pass_local = kv_ref.shape[1]
    _, group = row_parts(iota((rows, 1), 0))
    passage = recv_ref[:, 2 * HD : 3 * HD].astype(F32)
    lane = iota((rows, HD), 1).astype(F32)
    member = jnp.where((group == 2) & (passage == lane), 1.0, 0.0)
    lower = jnp.where(iota((rows, rows), 1) < iota((rows, rows), 0), 1.0, 0.0).astype(BF)
    rank = dot(lower, member.astype(BF))
    counts = jnp.sum(member, axis=0, keepdims=True)
    chunks = jnp.floor((counts + (CHUNK - 1)) * (1.0 / CHUNK))
    upto = jnp.where(iota((HD, HD), 0) <= iota((HD, HD), 1), 1.0, 0.0).astype(BF)
    ends = dot(jnp.broadcast_to(chunks, (8, HD)).astype(BF), upto)[0:1, :]
    firsts = ends - chunks
    place = jnp.sum(member * (rank + CHUNK * firsts), axis=1, keepdims=True)
    one = pltpu.roll(jnp.broadcast_to(place, (rows, HD)), rows - SLOTS, 0)
    two = pltpu.roll(jnp.broadcast_to(place, (rows, HD)), rows - 2 * SLOTS, 0)
    place = jnp.where(group == 0, two, jnp.where(group == 1, one, place))
    place = jnp.where(group < 3, place, -1.0)
    place_row = jnp.transpose(place)[0:1, :]
    _, group_row = row_parts(iota((1, rows), 1))
    target = iota((places, 1), 0).astype(F32)
    for g in range(3):
        pick = jnp.where(target == jnp.where(group_row == g, place_row, -2.0), 1.0, 0.0).astype(BF)
        sorted_ref[:, g * WIDE : (g + 1) * WIDE] = dot(pick, recv_ref[...]).astype(BF)
    result_ref[n_chunks * CHUNK :, :] = jnp.zeros(
        (places - n_chunks * CHUNK, result_ref.shape[1]), BF
    )
    limits = jnp.where(iota((1, HD), 1) < pass_local, ends, 1e9)
    lanes = iota((CHUNK, HD), 1)
    head_lane = jnp.bitwise_and(lanes, GROUP - 1)

    def attend(c, carry):
        index = jnp.sum(jnp.where(limits <= c.astype(F32), 1.0, 0.0)).astype(jnp.int32)
        index = jnp.minimum(index, pass_local - 1)
        at = pl.ds(pl.multiple_of(c * CHUNK, CHUNK), CHUNK)
        queries = jnp.concatenate(
            [sorted_ref[at, h * HD : (h + 1) * HD] for h in range(GROUP)], axis=0
        )
        scores = lax.dot_general(
            queries, kv_ref[0, index], (((1,), (1,)), ((), ())), preferred_element_type=F32
        )
        highest = jnp.max(scores, axis=1, keepdims=True)
        terms = jnp.exp2((scores - highest) * (SCALE * 1.4426950408889634))
        total = jnp.sum(terms, axis=1, keepdims=True)
        mixed = dot(terms.astype(BF), kv_ref[1, index]) * (1.0 / total)
        lse = highest * SCALE + jnp.log(total)
        sums = jnp.zeros((CHUNK, HD), F32)
        for h in range(GROUP):
            part = slice(h * CHUNK, (h + 1) * CHUNK)
            result_ref[at, h * HD : (h + 1) * HD] = mixed[part].astype(BF)
            sums = jnp.where(head_lane == h, lse[part], sums)
        high = sums.astype(BF).astype(F32)
        middle = (sums - high).astype(BF).astype(F32)
        low = sums - high - middle
        sums = jnp.where(lanes < GROUP, high, jnp.where(lanes < 2 * GROUP, middle, low))
        result_ref[at, GROUP * HD :] = sums.astype(BF)
        return carry

    lax.fori_loop(0, n_chunks, attend, 0, unroll=4)
    home = jnp.where(
        jnp.broadcast_to(place[:, 0:1], (rows, places)) == iota((rows, places), 1).astype(F32),
        1.0,
        0.0,
    ).astype(BF)
    back = dot(home, result_ref[:, 2 * WIDE : 3 * WIDE])
    back = jnp.where(group == 1, dot(home, result_ref[:, WIDE : 2 * WIDE]), back)
    back = jnp.where(group == 0, dot(home, result_ref[:, 0:WIDE]), back)
    back_ref[...] = back.astype(BF)


def project_kernel(
    stores,
    tps,
    y_chips,
    pass_local,
    q_ref,
    new_ref,
    id_ref,
    back_ref,
    w_ref,
    res_ref,
    out_ref,
    home,
    block,
    weight,
    part,
    others,
    total,
    final,
    ex_send,
    ex_recv,
    w_send,
    w_recv,
    right_send,
    right_recv,
    left_send,
    left_recv,
    sum_send,
    sum_recv,
    end_send,
    end_recv,
):
    me, tp = lax.axis_index("store"), lax.axis_index("tp")
    zs = stores // y_chips
    z = lax.div(me, y_chips)
    y = me - z * y_chips
    streams, width = q_ref.shape
    w_cols = w_ref.shape[1]
    cut = width // tps
    diagonal = z == tp
    barrier = pltpu.get_barrier_semaphore()

    def greet(device):
        pl.semaphore_signal(barrier, inc=1, device_id=device, device_id_type=MESH)

    def greet_store(k, carry):
        greet((lax.rem(me + k, stores), tp))
        return carry

    lax.fori_loop(1, stores, greet_store, 0)
    for k in range(1, tps):
        greet((me, lax.rem(tp + k, tps)))
    for other in range(tps):

        @pl.when(jnp.logical_not(diagonal & (tp == other)))
        def _():
            greet((tp * y_chips + y, other))

    pl.semaphore_wait(barrier, stores + 2 * tps - 2 - diagonal.astype(jnp.int32))

    def start(k, carry):
        exchange_copy(k, me, tp, stores, back_ref, home, ex_send, ex_recv).start()
        return carry

    lax.fori_loop(1, stores, start, 0)
    weight_copies = []
    for k in range(1, y_chips):
        copy = remote(
            w_ref,
            weight.at[y],
            w_send.at[k],
            w_recv.at[k],
            (z * y_chips + lax.rem(y + k, y_chips), tp),
        )
        copy.start()
        weight_copies.append(copy)
    mine = pl.ds(pl.multiple_of(me * BLOCK, BLOCK), BLOCK)
    home[mine, :] = back_ref[mine, :]
    weight[y] = w_ref[...]

    slot, _ = stream_slots(id_ref[...], pass_local)
    rows = stores * BLOCK
    row_slot, row_group = row_parts(iota((1, rows), 1))
    match = slot[0:streams] == row_slot.astype(F32)
    picks = [jnp.where(match & (row_group == g), 1.0, 0.0).astype(BF) for g in range(3)]
    new_key = new_ref[0].astype(F32)
    new_value = new_ref[1].astype(F32)
    own = [
        jnp.sum(q_ref[:, h * HD : (h + 1) * HD].astype(F32) * new_key, axis=1, keepdims=True)
        * SCALE
        for h in range(GROUP)
    ]

    def finish(k, carry):
        exchange_copy(k, me, tp, stores, back_ref, home, ex_send, ex_recv).wait()
        return carry

    lax.fori_loop(1, stores, finish, 0)
    got = [dot(pick, home[...]) for pick in picks]
    sums = got[2][:, 2 * HD : 3 * HD]
    for h in range(GROUP):
        g, b = divmod(h, 3)
        lse = sums[:, h : h + 1] + sums[:, GROUP + h : GROUP + h + 1]
        lse = lse + sums[:, 2 * GROUP + h : 2 * GROUP + h + 1]
        highest = jnp.maximum(lse, own[h])
        first = jnp.exp(lse - highest)
        second = jnp.exp(own[h] - highest)
        mixed = got[g][:, b * HD : (b + 1) * HD] * first + new_value * second
        block[z, :, h * HD : (h + 1) * HD] = (mixed * (1.0 / (first + second))).astype(BF)

    n_right, n_left = zs // 2, (zs - 1) // 2
    to_right = (lax.rem(z + 1, zs) * y_chips + y, tp)
    to_left = (lax.rem(z + zs - 1, zs) * y_chips + y, tp)

    def going_right(k):
        at = block.at[lax.rem(z + zs - k, zs)]
        return remote(at, at, right_send.at[k], right_recv.at[k], to_right)

    def going_left(k):
        at = block.at[lax.rem(z + k, zs)]
        return remote(at, at, left_send.at[k], left_recv.at[k], to_left)

    def came_right(k):
        at = block.at[lax.rem(z + zs - k - 1, zs)]
        return remote(at, at, right_send.at[k], right_recv.at[k], to_right)

    def came_left(k):
        at = block.at[lax.rem(z + k + 1, zs)]
        return remote(at, at, left_send.at[k], left_recv.at[k], to_left)

    if n_right:
        going_right(0).start()
    if n_left:
        going_left(0).start()
    for copy in weight_copies:
        copy.wait_recv()

    def sum_copy(i, k):
        to = lax.rem(tp + k, tps)
        return remote(
            part.at[i, to], others.at[i, tp], sum_send.at[i, k], sum_recv.at[i, k], (me, to)
        )

    def multiply(i, z_of):
        for v in range(y_chips):
            product = dot(block[z_of], weight[v])
            for u in range(w_cols // cut):
                part[i, v * (w_cols // cut) + u] = product[:, u * cut : (u + 1) * cut].astype(BF)
        for k in range(1, tps):
            sum_copy(i, k).start()

    def end_copy(i, z_of):
        return remote(
            total.at[i], final.at[tp], end_send.at[i], end_recv.at[tp], (z_of * y_chips + y, z)
        )

    def add_up(i, z_of):
        for k in range(1, tps):
            sum_copy(i, k).wait_recv()
        value = part[i, tp].astype(F32)
        for k in range(1, tps):
            value = value + others[i, lax.rem(tp + tps - k, tps)].astype(F32)
        total[i] = value.astype(BF)
        if i == 0:

            @pl.when(diagonal)
            def _():
                final[tp] = total[i]

            @pl.when(jnp.logical_not(diagonal))
            def _():
                end_copy(i, z_of).start()

        else:
            end_copy(i, z_of).start()

    order = [0]
    for k in range(1, n_right + 1):
        order.append(-k)
        if k <= n_left:
            order.append(k)
    where = [lax.rem(z + zs + o, zs) for o in order]
    lag = 2
    for i, o in enumerate(order):
        if o < 0:
            came_right(-o - 1).wait_recv()
            if -o < n_right:
                going_right(-o).start()
        elif o > 0:
            came_left(o - 1).wait_recv()
            if o < n_left:
                going_left(o).start()
        multiply(i, where[i])
        if i >= lag:
            add_up(i - lag, where[i - lag])
    for i in range(max(len(order) - lag, 0), len(order)):
        add_up(i, where[i])

    for other in range(tps):

        @pl.when(jnp.logical_not(diagonal & (tp == other)))
        def _():
            remote(
                total.at[0], final.at[other], end_send.at[0], end_recv.at[other], (me, tp)
            ).wait_recv()

        at = slice(other * cut, (other + 1) * cut)
        out_ref[:, at] = (res_ref[:, at].astype(F32) + final[other].astype(F32)).astype(BF)

    for copy in weight_copies:
        copy.wait_send()
    for k in range(n_right):
        going_right(k).wait_send()
    for k in range(n_left):
        going_left(k).wait_send()
    for i in range(zs):
        for k in range(1, tps):
            sum_copy(i, k).wait_send()
        if i == 0:

            @pl.when(jnp.logical_not(diagonal))
            def _():
                end_copy(i, where[i]).wait_send()

        else:
            end_copy(i, where[i]).wait_send()


def params(collective_id=None):
    return pltpu.CompilerParams(
        collective_id=collective_id,
        has_side_effects=collective_id is not None,
        vmem_limit_bytes=40 * 2**20,
    )


def shards(y_chips, query, new_kv, kv_store, passage_ids, residual_in, out_weight):
    stores, tps = lax.axis_size("store"), lax.axis_size("tp")
    zs = stores // y_chips
    streams, width = query.shape
    pass_local = kv_store.shape[1]
    rows = stores * BLOCK
    dma = pltpu.SemaphoreType.DMA
    received = pl.pallas_call(
        functools.partial(route_kernel, stores, pass_local),
        out_shape=jax.ShapeDtypeStruct((rows, WIDE), BF),
        in_specs=[VMEM] * 2,
        out_specs=VMEM,
        scratch_shapes=[
            pltpu.VMEM((PAD, 3 * WIDE), BF),
            pltpu.VMEM((rows, WIDE), BF),
            dma((stores,)),
            dma((stores,)),
        ],
        compiler_params=params(0),
        name="route",
    )(query, passage_ids)
    slots = stores * SLOTS
    n_chunks = (slots + pass_local * (CHUNK - 1)) // CHUNK
    places = -(-n_chunks * CHUNK // HD) * HD
    back = pl.pallas_call(
        functools.partial(attend_kernel, n_chunks),
        out_shape=jax.ShapeDtypeStruct((rows, WIDE), BF),
        in_specs=[VMEM] * 2,
        out_specs=VMEM,
        scratch_shapes=[
            pltpu.VMEM((places, 3 * WIDE), BF),
            pltpu.VMEM((places, 3 * WIDE), BF),
        ],
        compiler_params=params(),
        name="attend",
    )(received, kv_store)
    cut = width // tps
    return pl.pallas_call(
        functools.partial(project_kernel, stores, tps, y_chips, pass_local),
        out_shape=jax.ShapeDtypeStruct((streams, width), BF),
        in_specs=[VMEM] * 6,
        out_specs=VMEM,
        scratch_shapes=[
            pltpu.VMEM((rows, WIDE), BF),
            pltpu.VMEM((zs, streams, width), BF),
            pltpu.VMEM((y_chips, *out_weight.shape), BF),
            pltpu.VMEM((zs, tps, streams, cut), BF),
            pltpu.VMEM((zs, tps, streams, cut), BF),
            pltpu.VMEM((zs, streams, cut), BF),
            pltpu.VMEM((tps, streams, cut), BF),
            dma((stores,)),
            dma((stores,)),
            dma((y_chips,)),
            dma((y_chips,)),
            dma((zs,)),
            dma((zs,)),
            dma((zs,)),
            dma((zs,)),
            dma((zs, tps)),
            dma((zs, tps)),
            dma((zs,)),
            dma((tps,)),
        ],
        compiler_params=params(1),
        name="project",
    )(query, new_kv, passage_ids, back, out_weight, residual_in)


def solution(mesh, y_chips=Y_CHIPS):
    placed = (
        P("store", "tp"),
        P(None, "store", "tp"),
        P(None, "store", None, "tp"),
        P("store", None),
        P("store", "tp"),
        P("tp", "store"),
    )
    return jax.shard_map(
        functools.partial(shards, y_chips),
        mesh=mesh,
        in_specs=placed,
        out_specs=P("store", "tp"),
        check_vma=False,
    )
```

```python
import functools

import jax
import jax.numpy as jnp
import numpy as np
from jax import lax
from jax.experimental import pallas as pl
from jax.experimental.pallas import tpu as pltpu
from jax.sharding import PartitionSpec as P

HD = 128
PLEN = 512
GROUP = 8
SLOTS = 5
BLOCK = 16
WIDE = 3 * HD
PAD = 128
CHUNK = 16
Y_CHIPS = 4
TILES = (2, 0, 1)
MESH = pl.DeviceIdType.MESH
BF = jnp.bfloat16
F32 = jnp.float32
SCALE = 1.0 / HD**0.5
VMEM = pl.BlockSpec(memory_space=pltpu.VMEM)
HEADS = tuple(3 * g + b for b in TILES for g in range(3) if 3 * g + b < GROUP)
PIECES = GROUP
HBM = pl.BlockSpec(memory_space=pltpu.HBM)


def iota(shape, dim):
    return lax.broadcasted_iota(jnp.int32, shape, dim)


def dot(a, b):
    return jnp.dot(a, b, preferred_element_type=F32)


def row_parts(k):
    inner = jnp.bitwise_and(k, BLOCK - 1)
    group = (
        (inner >= SLOTS).astype(jnp.int32)
        + (inner >= 2 * SLOTS).astype(jnp.int32)
        + (inner >= 3 * SLOTS).astype(jnp.int32)
    )
    slot = jnp.right_shift(k, 4) * SLOTS + inner - SLOTS * group
    return slot, group


def as_row(column):
    return jnp.transpose(jnp.broadcast_to(column, (column.shape[0], HD)))[0:1, :]


def stream_slots(ids, pass_local):
    rows, width = ids.shape
    stream = iota((PAD, width), 0)
    spread = jnp.zeros((PAD, width), F32)
    place = jnp.full((PAD, width), -1, jnp.int32)
    for r in range(rows):
        inside = (stream >= r * width) & (stream < (r + 1) * width)
        spread = jnp.where(inside, ids[r : r + 1, :].astype(F32), spread)
        place = jnp.where(inside, stream - r * width, place)
    hit = place == iota((PAD, width), 1)
    passage = jnp.sum(jnp.where(hit, spread, 0.0), axis=1, keepdims=True)
    real = iota((PAD, 1), 0) < rows * width
    owner = jnp.floor((passage + 0.5) * (1.0 / pass_local))
    local = jnp.where(real, passage - owner * pass_local, 0.0)
    owner = jnp.where(real, owner, -1.0)
    same = owner == as_row(owner)
    earlier = iota((PAD, PAD), 1) < iota((PAD, PAD), 0)
    position = jnp.sum(jnp.where(same & earlier, 1.0, 0.0), axis=1, keepdims=True)
    return jnp.where(real, owner * SLOTS + position, -1.0), local


def remote(src, dst, send, recv, device):
    return pltpu.make_async_remote_copy(
        src_ref=src, dst_ref=dst, send_sem=send, recv_sem=recv, device_id=device, device_id_type=MESH
    )


def outward(k, stores):
    odd = jnp.bitwise_and(k, 1)
    return stores // 2 + jnp.where(odd == 1, lax.div(k, 2), -lax.div(k, 2))


def exchange_copy(k, me, tp, stores, msg, recv, send_sem, recv_sem):
    to = lax.rem(me + outward(k, stores), stores)
    return remote(
        msg.at[pl.ds(pl.multiple_of(to * BLOCK, BLOCK), BLOCK)],
        recv.at[pl.ds(pl.multiple_of(me * BLOCK, BLOCK), BLOCK)],
        send_sem.at[k],
        recv_sem.at[k],
        (to, tp),
    )


def pack(stores, slot, wide_ref, msg_ref):
    rows = stores * BLOCK
    row_slot, row_group = row_parts(iota((rows, 1), 0))
    wanted = jnp.where(row_group < 3, row_slot, -2).astype(F32)
    pick = jnp.where(wanted == as_row(slot), 1.0, 0.0).astype(BF)
    message = dot(pick, wide_ref[:, 2 * WIDE : 3 * WIDE])
    message = jnp.where(row_group == 1, dot(pick, wide_ref[:, WIDE : 2 * WIDE]), message)
    message = jnp.where(row_group == 0, dot(pick, wide_ref[:, 0:WIDE]), message)
    msg_ref[...] = message.astype(BF)


def sort_slots(n_chunks, pass_local, recv_ref, lower_ref, sorted_ref):
    rows = recv_ref.shape[0]
    places = sorted_ref.shape[0]
    _, group = row_parts(iota((rows, 1), 0))
    passage = recv_ref[:, 2 * HD : 3 * HD].astype(F32)
    lane = iota((rows, HD), 1).astype(F32)
    member = jnp.where((group == 2) & (passage == lane), 1.0, 0.0)
    rank = dot(lower_ref[...], member.astype(BF))
    counts = jnp.sum(member, axis=0, keepdims=True)
    chunks = jnp.floor((counts + (CHUNK - 1)) * (1.0 / CHUNK))
    upto = jnp.where(iota((HD, HD), 0) <= iota((HD, HD), 1), 1.0, 0.0).astype(BF)
    ends = dot(jnp.broadcast_to(chunks, (8, HD)).astype(BF), upto)[0:1, :]
    firsts = ends - chunks
    place = jnp.sum(member * (rank + CHUNK * firsts), axis=1, keepdims=True)
    one = pltpu.roll(jnp.broadcast_to(place, (rows, HD)), rows - SLOTS, 0)
    two = pltpu.roll(jnp.broadcast_to(place, (rows, HD)), rows - 2 * SLOTS, 0)
    place = jnp.where(group == 0, two, jnp.where(group == 1, one, place))
    place = jnp.where(group < 3, place, -1.0)
    place_row = jnp.transpose(place)[0:1, :]
    _, group_row = row_parts(iota((1, rows), 1))
    target = iota((places, 1), 0).astype(F32)
    for g in range(3):
        pick = jnp.where(target == jnp.where(group_row == g, place_row, -2.0), 1.0, 0.0).astype(BF)
        sorted_ref[:, g * WIDE : (g + 1) * WIDE] = dot(pick, recv_ref[...]).astype(BF)
    return place, jnp.where(iota((1, HD), 1) < pass_local, ends, 1e9)


def attend_chunks(n_chunks, pass_local, limits, sorted_ref, kv_ref, result_ref):
    lanes = iota((CHUNK, HD), 1)
    head_lane = jnp.bitwise_and(lanes, GROUP - 1)
    across = (((1,), (1,)), ((), ()))
    down = (((0,), (0,)), ((), ()))

    def attend(c, carry):
        index = jnp.sum(jnp.where(limits <= c.astype(F32), 1.0, 0.0)).astype(jnp.int32)
        index = jnp.clip(index, 0, pass_local - 1)
        at = pl.ds(pl.multiple_of(c * CHUNK, CHUNK), CHUNK)
        queries = jnp.concatenate(
            [sorted_ref[at, h * HD : (h + 1) * HD] for h in range(GROUP)], axis=0
        )
        scores = lax.dot_general(kv_ref[0, index], queries, across, preferred_element_type=F32)
        highest = jnp.max(scores, axis=0, keepdims=True)
        terms = jnp.exp2((scores - highest) * (SCALE * 1.4426950408889634))
        total = jnp.sum(terms, axis=0, keepdims=True)
        mixed = lax.dot_general(
            kv_ref[1, index], terms.astype(BF), down, preferred_element_type=F32
        )
        mixed = jnp.transpose(mixed * (1.0 / total))
        lse = highest * SCALE + jnp.log(total)
        lse = jnp.transpose(jnp.broadcast_to(lse, (8, GROUP * CHUNK)))[:, 0:1]
        sums = jnp.zeros((CHUNK, HD), F32)
        for h in range(GROUP):
            part = slice(h * CHUNK, (h + 1) * CHUNK)
            result_ref[at, h * HD : (h + 1) * HD] = mixed[part].astype(BF)
            sums = jnp.where(head_lane == h, lse[part], sums)
        high = sums.astype(BF).astype(F32)
        middle = (sums - high).astype(BF).astype(F32)
        low = sums - high - middle
        sums = jnp.where(lanes < GROUP, high, jnp.where(lanes < 2 * GROUP, middle, low))
        result_ref[at, GROUP * HD :] = sums.astype(BF)
        return carry

    lax.fori_loop(0, n_chunks, attend, 0, unroll=14)


def unsort(home, group, tile, result_ref, back_ref):
    back = dot(home, result_ref[:, (6 + tile) * HD : (7 + tile) * HD])
    back = jnp.where(group == 1, dot(home, result_ref[:, (3 + tile) * HD : (4 + tile) * HD]), back)
    back = jnp.where(group == 0, dot(home, result_ref[:, tile * HD : (tile + 1) * HD]), back)
    back_ref[tile] = back.astype(BF)


def kernel(
    stores,
    tps,
    y_chips,
    pass_local,
    n_chunks,
    q_hbm,
    new_hbm,
    kv_hbm,
    id_hbm,
    res_hbm,
    w_hbm,
    out_ref,
    q_ref,
    new_ref,
    kv_ref,
    id_ref,
    res_ref,
    wide,
    msg,
    recv,
    lower,
    sorted_ref,
    result,
    back,
    home,
    block,
    weight,
    part,
    pair,
    both,
    others,
    total,
    final,
    load_sem,
    go_send,
    go_recv,
    ex_send,
    ex_recv,
    w_send,
    w_recv,
    right_send,
    right_recv,
    left_send,
    left_recv,
    pair_send,
    pair_recv,
    sum_send,
    sum_recv,
    end_send,
    end_recv,
):
    me, tp = lax.axis_index("store"), lax.axis_index("tp")
    zs = stores // y_chips
    z = lax.div(me, y_chips)
    y = me - z * y_chips
    streams, width = q_ref.shape
    w_cols = w_hbm.shape[1]
    cut = width // tps
    diagonal = z == tp
    barrier = pltpu.get_barrier_semaphore()

    def greet(device):
        pl.semaphore_signal(barrier, inc=1, device_id=device, device_id_type=MESH)

    def greet_store(k, carry):
        greet((lax.rem(me + outward(k, stores), stores), tp))
        return carry

    lax.fori_loop(1, stores, greet_store, 0)
    for k in range(1, tps):
        greet((me, lax.rem(tp + k, tps)))
    for other in range(tps):

        @pl.when(jnp.logical_not(diagonal & (tp == other)))
        def _():
            greet((tp * y_chips + y, other))

    loads = [
        pltpu.make_async_copy(src, dst, load_sem.at[i])
        for i, (src, dst) in enumerate(
            [
                (id_hbm, id_ref),
                (q_hbm, q_ref),
                (kv_hbm, kv_ref),
                (new_hbm, new_ref),
                (res_hbm, res_ref),
                (w_hbm, weight.at[y]),
            ]
        )
    ]
    for load in loads:
        load.start()

    loads[0].wait()
    slot, local = stream_slots(id_ref[...], pass_local)
    wide[streams:, 0:width] = jnp.zeros((PAD - streams, width), BF)
    wide[:, width:] = jnp.broadcast_to(local, (PAD, HD)).astype(BF)
    loads[1].wait()
    wide[0:streams, 0:width] = q_ref[...]
    pack(stores, slot, wide, msg)
    pl.semaphore_wait(barrier, stores + 2 * tps - 2 - diagonal.astype(jnp.int32))

    def go(k, carry):
        exchange_copy(k, me, tp, stores, msg, recv, go_send, go_recv).start()
        return carry

    def went(k, carry):
        exchange_copy(k, me, tp, stores, msg, recv, go_send, go_recv).wait()
        return carry

    lax.fori_loop(1, stores, go, 0)
    above = (z * y_chips + lax.rem(y + 1, y_chips), tp)
    below = (z * y_chips + lax.rem(y + y_chips - 1, y_chips), tp)
    middle = w_hbm.shape[0] // 2

    def weight_up(came):
        return remote(
            w_hbm,
            weight.at[lax.rem(y + y_chips - 1, y_chips) if came else y],
            w_send.at[0],
            w_recv.at[0],
            above,
        )

    def weight_down(came):
        return remote(
            w_hbm,
            weight.at[lax.rem(y + 1, y_chips) if came else y],
            w_send.at[1],
            w_recv.at[1],
            below,
        )

    def half_up(came):
        at = weight.at[lax.rem(y + y_chips - (2 if came else 1), y_chips), 0:middle]
        return remote(at, at, w_send.at[2], w_recv.at[2], above)

    def half_down(came):
        at = weight.at[lax.rem(y + (2 if came else 1), y_chips), middle:]
        return remote(at, at, w_send.at[3], w_recv.at[3], below)

    near = [weight_up, weight_down][: y_chips - 1]
    far = [half_up, half_down] if y_chips > 3 else []
    for copy in near:
        copy(False).start()

    mine = pl.ds(pl.multiple_of(me * BLOCK, BLOCK), BLOCK)
    recv[mine, :] = msg[mine, :]
    rows = stores * BLOCK
    lower[...] = jnp.where(iota((rows, rows), 1) < iota((rows, rows), 0), 1.0, 0.0).astype(BF)
    result[n_chunks * CHUNK :, :] = jnp.zeros(
        (result.shape[0] - n_chunks * CHUNK, result.shape[1]), BF
    )
    loads[3].wait()
    new_key = new_ref[0].astype(F32)
    new_value = new_ref[1].astype(F32)
    own = [
        jnp.sum(q_ref[:, h * HD : (h + 1) * HD].astype(F32) * new_key, axis=1, keepdims=True)
        * SCALE
        for h in range(GROUP)
    ]
    loads[2].wait()
    lax.fori_loop(1, stores, went, 0)

    place, limits = sort_slots(n_chunks, pass_local, recv, lower, sorted_ref)
    attend_chunks(n_chunks, pass_local, limits, sorted_ref, kv_ref, result)
    for copy in near:
        copy(True).wait_recv()
    for copy in far:
        copy(False).start()
    places = result.shape[0]
    spread = jnp.broadcast_to(place[:, 0:1], (rows, places))
    send_home = jnp.where(spread == iota((rows, places), 1).astype(F32), 1.0, 0.0).astype(BF)
    _, group = row_parts(iota((rows, 1), 0))

    def give(tile, k, carry):
        exchange_copy(
            k, me, tp, stores, back.at[tile], home.at[tile], ex_send.at[tile], ex_recv.at[tile]
        ).start()
        return carry

    def given(tile, k, carry):
        exchange_copy(
            k, me, tp, stores, back.at[tile], home.at[tile], ex_send.at[tile], ex_recv.at[tile]
        ).wait()
        return carry

    for tile in TILES:
        unsort(send_home, group, tile, result, back)
        lax.fori_loop(1, stores, functools.partial(give, tile), 0)
        home[tile, mine, :] = back[tile, mine, :]
    row_slot, row_group = row_parts(iota((1, rows), 1))
    match = slot[0:streams] == row_slot.astype(F32)
    picks = [jnp.where(match & (row_group == g), 1.0, 0.0).astype(BF) for g in range(3)]

    half = zs // 2
    to_right = (lax.rem(z + 1, zs) * y_chips + y, tp)
    to_left = (lax.rem(z + zs - 1, zs) * y_chips + y, tp)

    def on_right(k, c):
        return k < half or (k == half and c < PIECES // 2)

    def on_left(k, c):
        return k < half or (k == half and c >= PIECES // 2)

    def right(k, c, came):
        at = block.at[lax.rem(z + zs - (k if came else k - 1), zs), c]
        return remote(at, at, right_send.at[k - 1, c], right_recv.at[k - 1, c], to_right)

    def left(k, c, came):
        at = block.at[lax.rem(z + (k if came else k - 1), zs), c]
        return remote(at, at, left_send.at[k - 1, c], left_recv.at[k - 1, c], to_left)

    def pass_on(k, c):
        if on_right(k, c):
            right(k, c, False).start()
        if on_left(k, c):
            left(k, c, False).start()

    for tile in TILES:
        lax.fori_loop(1, stores, functools.partial(given, tile), 0)
        if tile == 2:
            sums = dot(picks[2], home[tile])
        for h in range(tile, GROUP, 3):
            lse = sums[:, h : h + 1] + sums[:, GROUP + h : GROUP + h + 1]
            lse = lse + sums[:, 2 * GROUP + h : 2 * GROUP + h + 1]
            highest = jnp.maximum(lse, own[h])
            first = jnp.exp(lse - highest)
            second = jnp.exp(own[h] - highest)
            mixed = dot(picks[h // 3], home[tile]) * first + new_value * second
            piece = HEADS.index(h)
            block[z, piece] = (mixed * (1.0 / (first + second))).astype(BF)
            pass_on(1, piece)

    xs = tps // 2
    x = lax.div(tp, 2)
    core = tp - 2 * x

    def pair_copy(i):
        return remote(
            part.at[i, 1 - core], pair.at[i], pair_send.at[i], pair_recv.at[i], (me, 2 * x + 1 - core)
        )

    def sum_copy(i, k):
        to = lax.rem(x + k, xs)
        return remote(
            both.at[i, to], others.at[i, x], sum_send.at[i, k], sum_recv.at[i, k], (me, 2 * to + core)
        )

    def multiply(i):
        for v in range(y_chips):
            product = sum(
                dot(block[where[i], piece], weight[v, h * HD : (h + 1) * HD, :])
                for piece, h in enumerate(HEADS)
            )
            for u in range(w_cols // cut):
                column = v * (w_cols // cut) + u
                part[i, column % 2, column // 2] = product[:, u * cut : (u + 1) * cut].astype(BF)
        pair_copy(i).start()

    def across(i):
        pair_copy(i).wait_recv()
        both[i] = (part[i, core].astype(F32) + pair[i].astype(F32)).astype(BF)
        for k in range(1, xs):
            sum_copy(i, k).start()

    def end_copy(i):
        return remote(
            total.at[i],
            final.at[tp],
            end_send.at[i],
            end_recv.at[tp],
            (where[i] * y_chips + y, z),
        )

    def add_up(i):
        value = part[i, core, x].astype(F32)
        for k in range(1, xs):
            sum_copy(i, k).wait_recv()
        value = value + pair[i, x].astype(F32)
        for k in range(1, xs):
            value = value + others[i, lax.rem(x + xs - k, xs)].astype(F32)
        total[i] = value.astype(BF)
        if i == 0:

            @pl.when(diagonal)
            def _():
                final[tp] = total[i]

            @pl.when(jnp.logical_not(diagonal))
            def _():
                end_copy(i).start()

        else:
            end_copy(i).start()

    offsets = [0]
    for k in range(1, half):
        offsets += [-k, k]
    offsets.append(-half)
    where = [lax.rem(z + zs + o, zs) for o in offsets]
    loads[5].wait()
    for copy in far:
        copy(True).wait_recv()
    ready = [[0]] + [[2 * k - 1, 2 * k] for k in range(1, half)] + [[zs - 1]]
    for k in range(1, half + 1):
        tasks = [
            [functools.partial(step, i) for i in (ready[k - lag] if k >= lag else [])]
            for lag, step in ((1, multiply), (2, across), (3, add_up))
        ]
        for c in range(PIECES):
            if on_right(k, c):
                right(k, c, True).wait_recv()
                if on_right(k + 1, c):
                    right(k + 1, c, False).start()
            if on_left(k, c):
                left(k, c, True).wait_recv()
                if on_left(k + 1, c):
                    left(k + 1, c, False).start()
            if c < len(tasks):
                for task in tasks[c]:
                    task()
    for i in ready[half - 1]:
        across(i)
    multiply(zs - 1)
    for i in ready[half]:
        across(i)
    for blocks in ready[max(half - 2, 0) :]:
        for i in blocks:
            add_up(i)

    loads[4].wait()
    for other in range(tps):

        @pl.when(jnp.logical_not(diagonal & (tp == other)))
        def _():
            remote(
                total.at[0], final.at[other], end_send.at[0], end_recv.at[other], (me, tp)
            ).wait_recv()

        at = slice(other * cut, (other + 1) * cut)
        out_ref[:, at] = (res_ref[:, at].astype(F32) + final[other].astype(F32)).astype(BF)

    for copy in near + far:
        copy(False).wait_send()
    for k in range(1, half + 1):
        for c in range(PIECES):
            if on_right(k, c):
                right(k, c, False).wait_send()
            if on_left(k, c):
                left(k, c, False).wait_send()
    for i in range(zs):
        pair_copy(i).wait_send()
        for k in range(1, xs):
            sum_copy(i, k).wait_send()
        if i == 0:

            @pl.when(jnp.logical_not(diagonal))
            def _():
                end_copy(i).wait_send()

        else:
            end_copy(i).wait_send()


def shards(y_chips, query, new_kv, kv_store, passage_ids, residual_in, out_weight):
    stores, tps = lax.axis_size("store"), lax.axis_size("tp")
    zs = stores // y_chips
    streams, width = query.shape
    pass_local = kv_store.shape[1]
    rows = stores * BLOCK
    n_chunks = (stores * SLOTS + pass_local * (CHUNK - 1)) // CHUNK
    places = -(-n_chunks * CHUNK // HD) * HD
    cut = width // tps
    dma = pltpu.SemaphoreType.DMA

    def vmem(*shape):
        return pltpu.VMEM(shape, BF)

    return pl.pallas_call(
        functools.partial(kernel, stores, tps, y_chips, pass_local, n_chunks),
        out_shape=pltpu.VMEM((streams, width), BF),
        in_specs=[HBM] * 6,
        out_specs=VMEM,
        scratch_shapes=[
            vmem(streams, width),
            vmem(*new_kv.shape),
            vmem(*kv_store.shape),
            pltpu.VMEM(passage_ids.shape, jnp.int32),
            vmem(streams, width),
            vmem(PAD, 3 * WIDE),
            vmem(rows, WIDE),
            vmem(rows, WIDE),
            vmem(rows, rows),
            vmem(places, 3 * WIDE),
            vmem(places, 3 * WIDE),
            vmem(3, rows, HD),
            vmem(3, rows, HD),
            vmem(zs, PIECES, streams, width // PIECES),
            vmem(y_chips, *out_weight.shape),
            vmem(zs, 2, tps // 2, streams, cut),
            vmem(zs, tps // 2, streams, cut),
            vmem(zs, tps // 2, streams, cut),
            vmem(zs, tps // 2, streams, cut),
            vmem(zs, streams, cut),
            vmem(tps, streams, cut),
            dma((6,)),
            dma((stores,)),
            dma((stores,)),
            dma((3, stores)),
            dma((3, stores)),
            dma((4,)),
            dma((4,)),
            dma((zs // 2, PIECES)),
            dma((zs // 2, PIECES)),
            dma((zs // 2, PIECES)),
            dma((zs // 2, PIECES)),
            dma((zs,)),
            dma((zs,)),
            dma((zs, tps // 2)),
            dma((zs, tps // 2)),
            dma((zs,)),
            dma((tps,)),
        ],
        compiler_params=pltpu.CompilerParams(
            collective_id=0, has_side_effects=True, vmem_limit_bytes=48 * 2**20
        ),
        name="decode",
    )(*[pltpu.with_memory_space_constraint(a, pltpu.HBM) for a in (query, new_kv, kv_store, passage_ids, residual_in, out_weight)])


def solution(mesh, y_chips=Y_CHIPS):
    placed = (
        P("store", "tp"),
        P(None, "store", "tp"),
        P(None, "store", None, "tp"),
        P("store", None),
        P("store", "tp"),
        P("tp", "store"),
    )
    return jax.shard_map(
        functools.partial(shards, y_chips),
        mesh=mesh,
        in_specs=placed,
        out_specs=P("store", "tp"),
        check_vma=False,
    )
```

```python
import functools

import jax
import jax.numpy as jnp
import numpy as np
from jax import lax
from jax.experimental import pallas as pl
from jax.experimental.pallas import tpu as pltpu
from jax.sharding import PartitionSpec as P

HD = 128
PLEN = 512
GROUP = 8
SLOTS = 5
BLOCK = 16
WIDE = 3 * HD
PAD = 128
CHUNK = 16
Y_CHIPS = 4
TILES = (2, 0, 1)
MESH = pl.DeviceIdType.MESH
BF = jnp.bfloat16
F32 = jnp.float32
SCALE = 1.0 / HD**0.5
VMEM = pl.BlockSpec(memory_space=pltpu.VMEM)
HEADS = tuple(3 * g + b for b in TILES for g in range(3) if 3 * g + b < GROUP)
PIECES = GROUP
HBM = pl.BlockSpec(memory_space=pltpu.HBM)


def iota(shape, dim):
    return lax.broadcasted_iota(jnp.int32, shape, dim)


def dot(a, b):
    return jnp.dot(a, b, preferred_element_type=F32)


def row_parts(k):
    inner = jnp.bitwise_and(k, BLOCK - 1)
    group = (
        (inner >= SLOTS).astype(jnp.int32)
        + (inner >= 2 * SLOTS).astype(jnp.int32)
        + (inner >= 3 * SLOTS).astype(jnp.int32)
    )
    slot = jnp.right_shift(k, 4) * SLOTS + inner - SLOTS * group
    return slot, group


def as_row(column):
    return jnp.transpose(jnp.broadcast_to(column, (column.shape[0], HD)))[0:1, :]


def stream_slots(ids, pass_local):
    rows, width = ids.shape
    stream = iota((PAD, width), 0)
    spread = jnp.zeros((PAD, width), F32)
    place = jnp.full((PAD, width), -1, jnp.int32)
    for r in range(rows):
        inside = (stream >= r * width) & (stream < (r + 1) * width)
        spread = jnp.where(inside, ids[r : r + 1, :].astype(F32), spread)
        place = jnp.where(inside, stream - r * width, place)
    hit = place == iota((PAD, width), 1)
    passage = jnp.sum(jnp.where(hit, spread, 0.0), axis=1, keepdims=True)
    real = iota((PAD, 1), 0) < rows * width
    owner = jnp.floor((passage + 0.5) * (1.0 / pass_local))
    local = jnp.where(real, passage - owner * pass_local, 0.0)
    owner = jnp.where(real, owner, -1.0)
    same = owner == as_row(owner)
    earlier = iota((PAD, PAD), 1) < iota((PAD, PAD), 0)
    position = jnp.sum(jnp.where(same & earlier, 1.0, 0.0), axis=1, keepdims=True)
    return jnp.where(real, owner * SLOTS + position, -1.0), local


def remote(src, dst, send, recv, device):
    return pltpu.make_async_remote_copy(
        src_ref=src, dst_ref=dst, send_sem=send, recv_sem=recv, device_id=device, device_id_type=MESH
    )


def outward(k, stores):
    odd = jnp.bitwise_and(k, 1)
    return stores // 2 + jnp.where(odd == 1, lax.div(k, 2), -lax.div(k, 2))


def exchange_copy(k, me, tp, stores, msg, recv, send_sem, recv_sem):
    to = lax.rem(me + outward(k, stores), stores)
    return remote(
        msg.at[pl.ds(pl.multiple_of(to * BLOCK, BLOCK), BLOCK)],
        recv.at[pl.ds(pl.multiple_of(me * BLOCK, BLOCK), BLOCK)],
        send_sem.at[k],
        recv_sem.at[k],
        (to, tp),
    )


def pack(stores, slot, wide_ref, msg_ref):
    rows = stores * BLOCK
    row_slot, row_group = row_parts(iota((rows, 1), 0))
    wanted = jnp.where(row_group < 3, row_slot, -2).astype(F32)
    pick = jnp.where(wanted == as_row(slot), 1.0, 0.0).astype(BF)
    message = dot(pick, wide_ref[:, 2 * WIDE : 3 * WIDE])
    message = jnp.where(row_group == 1, dot(pick, wide_ref[:, WIDE : 2 * WIDE]), message)
    message = jnp.where(row_group == 0, dot(pick, wide_ref[:, 0:WIDE]), message)
    msg_ref[...] = message.astype(BF)


def sort_slots(n_chunks, pass_local, recv_ref, lower_ref, sorted_ref):
    rows = recv_ref.shape[0]
    places = sorted_ref.shape[0]
    _, group = row_parts(iota((rows, 1), 0))
    passage = recv_ref[:, 2 * HD : 3 * HD].astype(F32)
    lane = iota((rows, HD), 1).astype(F32)
    member = jnp.where((group == 2) & (passage == lane), 1.0, 0.0)
    rank = dot(lower_ref[...], member.astype(BF))
    counts = jnp.sum(member, axis=0, keepdims=True)
    chunks = jnp.floor((counts + (CHUNK - 1)) * (1.0 / CHUNK))
    upto = jnp.where(iota((HD, HD), 0) <= iota((HD, HD), 1), 1.0, 0.0).astype(BF)
    ends = dot(jnp.broadcast_to(chunks, (8, HD)).astype(BF), upto)[0:1, :]
    firsts = ends - chunks
    place = jnp.sum(member * (rank + CHUNK * firsts), axis=1, keepdims=True)
    one = pltpu.roll(jnp.broadcast_to(place, (rows, HD)), rows - SLOTS, 0)
    two = pltpu.roll(jnp.broadcast_to(place, (rows, HD)), rows - 2 * SLOTS, 0)
    place = jnp.where(group == 0, two, jnp.where(group == 1, one, place))
    place = jnp.where(group < 3, place, -1.0)
    place_row = jnp.transpose(place)[0:1, :]
    _, group_row = row_parts(iota((1, rows), 1))
    target = iota((places, 1), 0).astype(F32)
    for g in range(3):
        pick = jnp.where(target == jnp.where(group_row == g, place_row, -2.0), 1.0, 0.0).astype(BF)
        sorted_ref[:, g * WIDE : (g + 1) * WIDE] = dot(pick, recv_ref[...]).astype(BF)
    return place, jnp.where(iota((1, HD), 1) < pass_local, ends, 1e9)


def attend_chunks(n_chunks, pass_local, limits, sorted_ref, kv_ref, result_ref):
    lanes = iota((CHUNK, HD), 1)
    head_lane = jnp.bitwise_and(lanes, GROUP - 1)
    across = (((1,), (1,)), ((), ()))
    down = (((0,), (0,)), ((), ()))

    def attend(c, carry):
        index = jnp.sum(jnp.where(limits <= c.astype(F32), 1.0, 0.0)).astype(jnp.int32)
        index = jnp.clip(index, 0, pass_local - 1)
        at = pl.ds(pl.multiple_of(c * CHUNK, CHUNK), CHUNK)
        queries = jnp.concatenate(
            [sorted_ref[at, h * HD : (h + 1) * HD] for h in range(GROUP)], axis=0
        )
        scores = lax.dot_general(kv_ref[0, index], queries, across, preferred_element_type=F32)
        highest = jnp.max(scores, axis=0, keepdims=True)
        terms = jnp.exp2((scores - highest) * (SCALE * 1.4426950408889634))
        total = jnp.sum(terms, axis=0, keepdims=True)
        mixed = lax.dot_general(
            kv_ref[1, index], terms.astype(BF), down, preferred_element_type=F32
        )
        mixed = jnp.transpose(mixed * (1.0 / total))
        lse = highest * SCALE + jnp.log(total)
        lse = jnp.transpose(jnp.broadcast_to(lse, (8, GROUP * CHUNK)))[:, 0:1]
        sums = jnp.zeros((CHUNK, HD), F32)
        for h in range(GROUP):
            part = slice(h * CHUNK, (h + 1) * CHUNK)
            result_ref[at, h * HD : (h + 1) * HD] = mixed[part].astype(BF)
            sums = jnp.where(head_lane == h, lse[part], sums)
        high = sums.astype(BF).astype(F32)
        middle = (sums - high).astype(BF).astype(F32)
        low = sums - high - middle
        sums = jnp.where(lanes < GROUP, high, jnp.where(lanes < 2 * GROUP, middle, low))
        result_ref[at, GROUP * HD :] = sums.astype(BF)
        return carry

    lax.fori_loop(0, n_chunks, attend, 0, unroll=14)


def unsort(home, group, tile, result_ref, back_ref):
    back = dot(home, result_ref[:, (6 + tile) * HD : (7 + tile) * HD])
    back = jnp.where(group == 1, dot(home, result_ref[:, (3 + tile) * HD : (4 + tile) * HD]), back)
    back = jnp.where(group == 0, dot(home, result_ref[:, tile * HD : (tile + 1) * HD]), back)
    back_ref[tile] = back.astype(BF)


def kernel(
    stores,
    tps,
    y_chips,
    pass_local,
    n_chunks,
    q_hbm,
    new_hbm,
    kv_hbm,
    id_hbm,
    res_hbm,
    w_hbm,
    out_ref,
    q_ref,
    new_ref,
    kv_ref,
    id_ref,
    res_ref,
    wide,
    msg,
    recv,
    lower,
    sorted_ref,
    result,
    back,
    home,
    block,
    weight,
    part,
    pair,
    both,
    others,
    total,
    final,
    load_sem,
    go_send,
    go_recv,
    ex_send,
    ex_recv,
    w_send,
    w_recv,
    right_send,
    right_recv,
    left_send,
    left_recv,
    pair_send,
    pair_recv,
    sum_send,
    sum_recv,
    end_send,
    end_recv,
):
    me, tp = lax.axis_index("store"), lax.axis_index("tp")
    zs = stores // y_chips
    z = lax.div(me, y_chips)
    y = me - z * y_chips
    streams, width = q_ref.shape
    w_cols = w_hbm.shape[1]
    cut = width // tps
    diagonal = z == tp
    barrier = pltpu.get_barrier_semaphore()

    def greet(device):
        pl.semaphore_signal(barrier, inc=1, device_id=device, device_id_type=MESH)

    def greet_store(k, carry):
        greet((lax.rem(me + outward(k, stores), stores), tp))
        return carry

    lax.fori_loop(1, stores, greet_store, 0)
    for k in range(1, tps):
        greet((me, lax.rem(tp + k, tps)))
    for other in range(tps):

        @pl.when(jnp.logical_not(diagonal & (tp == other)))
        def _():
            greet((tp * y_chips + y, other))

    loads = [
        pltpu.make_async_copy(src, dst, load_sem.at[i])
        for i, (src, dst) in enumerate(
            [
                (id_hbm, id_ref),
                (q_hbm, q_ref),
                (kv_hbm, kv_ref),
                (new_hbm, new_ref),
                (res_hbm, res_ref),
                (w_hbm, weight.at[y]),
            ]
        )
    ]
    for load in loads:
        load.start()

    loads[0].wait()
    slot, local = stream_slots(id_ref[...], pass_local)
    wide[streams:, 0:width] = jnp.zeros((PAD - streams, width), BF)
    wide[:, width:] = jnp.broadcast_to(local, (PAD, HD)).astype(BF)
    loads[1].wait()
    wide[0:streams, 0:width] = q_ref[...]
    pack(stores, slot, wide, msg)
    pl.semaphore_wait(barrier, stores + 2 * tps - 2 - diagonal.astype(jnp.int32))

    def go(k, carry):
        exchange_copy(k, me, tp, stores, msg, recv, go_send, go_recv).start()
        return carry

    def went(k, carry):
        exchange_copy(k, me, tp, stores, msg, recv, go_send, go_recv).wait()
        return carry

    lax.fori_loop(1, stores, go, 0)
    above = (z * y_chips + lax.rem(y + 1, y_chips), tp)
    below = (z * y_chips + lax.rem(y + y_chips - 1, y_chips), tp)
    middle = w_hbm.shape[0] // 2

    def weight_up(came):
        return remote(
            w_hbm,
            weight.at[lax.rem(y + y_chips - 1, y_chips) if came else y],
            w_send.at[0],
            w_recv.at[0],
            above,
        )

    def weight_down(came):
        return remote(
            w_hbm,
            weight.at[lax.rem(y + 1, y_chips) if came else y],
            w_send.at[1],
            w_recv.at[1],
            below,
        )

    def half_up(came):
        at = weight.at[lax.rem(y + y_chips - (2 if came else 1), y_chips), 0:middle]
        return remote(at, at, w_send.at[2], w_recv.at[2], above)

    def half_down(came):
        at = weight.at[lax.rem(y + (2 if came else 1), y_chips), middle:]
        return remote(at, at, w_send.at[3], w_recv.at[3], below)

    near = [weight_up, weight_down][: y_chips - 1]
    far = [half_up, half_down] if y_chips > 3 else []
    for copy in near:
        copy(False).start()

    mine = pl.ds(pl.multiple_of(me * BLOCK, BLOCK), BLOCK)
    recv[mine, :] = msg[mine, :]
    rows = stores * BLOCK
    lower[...] = jnp.where(iota((rows, rows), 1) < iota((rows, rows), 0), 1.0, 0.0).astype(BF)
    result[n_chunks * CHUNK :, :] = jnp.zeros(
        (result.shape[0] - n_chunks * CHUNK, result.shape[1]), BF
    )
    loads[3].wait()
    new_key = new_ref[0].astype(F32)
    new_value = new_ref[1].astype(F32)
    own = [
        jnp.sum(q_ref[:, h * HD : (h + 1) * HD].astype(F32) * new_key, axis=1, keepdims=True)
        * SCALE
        for h in range(GROUP)
    ]
    loads[2].wait()
    lax.fori_loop(1, stores, went, 0)

    place, limits = sort_slots(n_chunks, pass_local, recv, lower, sorted_ref)
    attend_chunks(n_chunks, pass_local, limits, sorted_ref, kv_ref, result)
    for copy in near:
        copy(True).wait_recv()
    for copy in far:
        copy(False).start()
    places = result.shape[0]
    spread = jnp.broadcast_to(place[:, 0:1], (rows, places))
    send_home = jnp.where(spread == iota((rows, places), 1).astype(F32), 1.0, 0.0).astype(BF)
    _, group = row_parts(iota((rows, 1), 0))

    def give(tile, k, carry):
        exchange_copy(
            k, me, tp, stores, back.at[tile], home.at[tile], ex_send.at[tile], ex_recv.at[tile]
        ).start()
        return carry

    def given(tile, k, carry):
        exchange_copy(
            k, me, tp, stores, back.at[tile], home.at[tile], ex_send.at[tile], ex_recv.at[tile]
        ).wait()
        return carry

    for tile in TILES:
        unsort(send_home, group, tile, result, back)
        lax.fori_loop(1, stores, functools.partial(give, tile), 0)
        home[tile, mine, :] = back[tile, mine, :]
    row_slot, row_group = row_parts(iota((1, rows), 1))
    match = slot[0:streams] == row_slot.astype(F32)
    picks = [jnp.where(match & (row_group == g), 1.0, 0.0).astype(BF) for g in range(3)]

    half = zs // 2
    to_right = (lax.rem(z + 1, zs) * y_chips + y, tp)
    to_left = (lax.rem(z + zs - 1, zs) * y_chips + y, tp)

    def on_right(k, c):
        return k < half or (k == half and c < PIECES // 2)

    def on_left(k, c):
        return k < half or (k == half and c >= PIECES // 2)

    def right(k, c, came):
        at = block.at[lax.rem(z + zs - (k if came else k - 1), zs), c]
        return remote(at, at, right_send.at[k - 1, c], right_recv.at[k - 1, c], to_right)

    def left(k, c, came):
        at = block.at[lax.rem(z + (k if came else k - 1), zs), c]
        return remote(at, at, left_send.at[k - 1, c], left_recv.at[k - 1, c], to_left)

    def pass_on(k, c):
        if on_right(k, c):
            right(k, c, False).start()
        if on_left(k, c):
            left(k, c, False).start()

    for tile in TILES:
        lax.fori_loop(1, stores, functools.partial(given, tile), 0)
        if tile == 2:
            sums = dot(picks[2], home[tile])
        for h in range(tile, GROUP, 3):
            lse = sums[:, h : h + 1] + sums[:, GROUP + h : GROUP + h + 1]
            lse = lse + sums[:, 2 * GROUP + h : 2 * GROUP + h + 1]
            highest = jnp.maximum(lse, own[h])
            first = jnp.exp(lse - highest)
            second = jnp.exp(own[h] - highest)
            mixed = dot(picks[h // 3], home[tile]) * first + new_value * second
            piece = HEADS.index(h)
            block[z, piece] = (mixed * (1.0 / (first + second))).astype(BF)
            pass_on(1, piece)

    xs = tps // 2
    x = lax.div(tp, 2)
    core = tp - 2 * x

    def pair_copy(i):
        return remote(
            part.at[i, 1 - core], pair.at[i], pair_send.at[i], pair_recv.at[i], (me, 2 * x + 1 - core)
        )

    def sum_copy(i, k):
        to = lax.rem(x + k, xs)
        return remote(
            both.at[i, to], others.at[i, x], sum_send.at[i, k], sum_recv.at[i, k], (me, 2 * to + core)
        )

    def multiply(blocks):
        pieces = [
            jnp.concatenate([block[where[i], piece] for i in blocks], axis=0)
            for piece in range(PIECES)
        ]
        for v in range(y_chips):
            product = sum(
                dot(pieces[piece], weight[v, h * HD : (h + 1) * HD, :])
                for piece, h in enumerate(HEADS)
            )
            for n, i in enumerate(blocks):
                for u in range(w_cols // cut):
                    column = v * (w_cols // cut) + u
                    part[i, column % 2, column // 2] = product[
                        n * streams : (n + 1) * streams, u * cut : (u + 1) * cut
                    ].astype(BF)
        for i in blocks:
            pair_copy(i).start()

    def across(i):
        pair_copy(i).wait_recv()
        both[i] = (part[i, core].astype(F32) + pair[i].astype(F32)).astype(BF)
        for k in range(1, xs):
            sum_copy(i, k).start()

    def end_copy(i):
        return remote(
            total.at[i],
            final.at[tp],
            end_send.at[i],
            end_recv.at[tp],
            (where[i] * y_chips + y, z),
        )

    def add_up(i):
        value = part[i, core, x].astype(F32)
        for k in range(1, xs):
            sum_copy(i, k).wait_recv()
        value = value + pair[i, x].astype(F32)
        for k in range(1, xs):
            value = value + others[i, lax.rem(x + xs - k, xs)].astype(F32)
        total[i] = value.astype(BF)
        if i == 0:

            @pl.when(diagonal)
            def _():
                final[tp] = total[i]

            @pl.when(jnp.logical_not(diagonal))
            def _():
                end_copy(i).start()

        else:
            end_copy(i).start()

    offsets = [0]
    for k in range(1, half):
        offsets += [-k, k]
    offsets.append(-half)
    where = [lax.rem(z + zs + o, zs) for o in offsets]
    loads[5].wait()
    for copy in far:
        copy(True).wait_recv()
    ready = [[0]] + [[2 * k - 1, 2 * k] for k in range(1, half)] + [[zs - 1]]
    for k in range(1, half + 1):
        tasks = [functools.partial(multiply, ready[k - 1])]
        if k >= 2:
            tasks += [functools.partial(across, i) for i in ready[k - 2]]
        if k >= 3:
            tasks += [functools.partial(add_up, i) for i in ready[k - 3]]
        for c in range(PIECES):
            if on_right(k, c):
                right(k, c, True).wait_recv()
                if on_right(k + 1, c):
                    right(k + 1, c, False).start()
            if on_left(k, c):
                left(k, c, True).wait_recv()
                if on_left(k + 1, c):
                    left(k + 1, c, False).start()
            if c < len(tasks):
                tasks[c]()
    for i in ready[half - 1]:
        across(i)
    multiply(ready[half])
    for i in ready[half]:
        across(i)
    for blocks in ready[max(half - 2, 0) :]:
        for i in blocks:
            add_up(i)

    loads[4].wait()
    for other in range(tps):

        @pl.when(jnp.logical_not(diagonal & (tp == other)))
        def _():
            remote(
                total.at[0], final.at[other], end_send.at[0], end_recv.at[other], (me, tp)
            ).wait_recv()

        at = slice(other * cut, (other + 1) * cut)
        out_ref[:, at] = (res_ref[:, at].astype(F32) + final[other].astype(F32)).astype(BF)

    for copy in near + far:
        copy(False).wait_send()
    for k in range(1, half + 1):
        for c in range(PIECES):
            if on_right(k, c):
                right(k, c, False).wait_send()
            if on_left(k, c):
                left(k, c, False).wait_send()
    for i in range(zs):
        pair_copy(i).wait_send()
        for k in range(1, xs):
            sum_copy(i, k).wait_send()
        if i == 0:

            @pl.when(jnp.logical_not(diagonal))
            def _():
                end_copy(i).wait_send()

        else:
            end_copy(i).wait_send()


def shards(y_chips, query, new_kv, kv_store, passage_ids, residual_in, out_weight):
    stores, tps = lax.axis_size("store"), lax.axis_size("tp")
    zs = stores // y_chips
    streams, width = query.shape
    pass_local = kv_store.shape[1]
    rows = stores * BLOCK
    n_chunks = (stores * SLOTS + pass_local * (CHUNK - 1)) // CHUNK
    places = -(-n_chunks * CHUNK // HD) * HD
    cut = width // tps
    dma = pltpu.SemaphoreType.DMA

    def vmem(*shape):
        return pltpu.VMEM(shape, BF)

    return pl.pallas_call(
        functools.partial(kernel, stores, tps, y_chips, pass_local, n_chunks),
        out_shape=pltpu.VMEM((streams, width), BF),
        in_specs=[HBM] * 6,
        out_specs=VMEM,
        scratch_shapes=[
            vmem(streams, width),
            vmem(*new_kv.shape),
            vmem(*kv_store.shape),
            pltpu.VMEM(passage_ids.shape, jnp.int32),
            vmem(streams, width),
            vmem(PAD, 3 * WIDE),
            vmem(rows, WIDE),
            vmem(rows, WIDE),
            vmem(rows, rows),
            vmem(places, 3 * WIDE),
            vmem(places, 3 * WIDE),
            vmem(3, rows, HD),
            vmem(3, rows, HD),
            vmem(zs, PIECES, streams, width // PIECES),
            vmem(y_chips, *out_weight.shape),
            vmem(zs, 2, tps // 2, streams, cut),
            vmem(zs, tps // 2, streams, cut),
            vmem(zs, tps // 2, streams, cut),
            vmem(zs, tps // 2, streams, cut),
            vmem(zs, streams, cut),
            vmem(tps, streams, cut),
            dma((6,)),
            dma((stores,)),
            dma((stores,)),
            dma((3, stores)),
            dma((3, stores)),
            dma((4,)),
            dma((4,)),
            dma((zs // 2, PIECES)),
            dma((zs // 2, PIECES)),
            dma((zs // 2, PIECES)),
            dma((zs // 2, PIECES)),
            dma((zs,)),
            dma((zs,)),
            dma((zs, tps // 2)),
            dma((zs, tps // 2)),
            dma((zs,)),
            dma((tps,)),
        ],
        compiler_params=pltpu.CompilerParams(
            collective_id=0, has_side_effects=True, vmem_limit_bytes=48 * 2**20
        ),
        name="decode",
    )(*[pltpu.with_memory_space_constraint(a, pltpu.HBM) for a in (query, new_kv, kv_store, passage_ids, residual_in, out_weight)])


def solution(mesh, y_chips=Y_CHIPS):
    placed = (
        P("store", "tp"),
        P(None, "store", "tp"),
        P(None, "store", None, "tp"),
        P("store", None),
        P("store", "tp"),
        P("tp", "store"),
    )
    return jax.shard_map(
        functools.partial(shards, y_chips),
        mesh=mesh,
        in_specs=placed,
        out_specs=P("store", "tp"),
        check_vma=False,
    )
```

```python
import functools

import jax
import jax.numpy as jnp
import numpy as np
from jax import lax
from jax.experimental import pallas as pl
from jax.experimental.pallas import tpu as pltpu
from jax.sharding import PartitionSpec as P

HD = 128
PLEN = 512
GROUP = 8
SLOTS = 5
BLOCK = 16
WIDE = 3 * HD
PAD = 128
CHUNK = 16
Y_CHIPS = 4
TILES = (2, 0, 1)
MESH = pl.DeviceIdType.MESH
BF = jnp.bfloat16
F32 = jnp.float32
SCALE = 1.0 / HD**0.5
VMEM = pl.BlockSpec(memory_space=pltpu.VMEM)
HEADS = tuple(3 * g + b for b in TILES for g in range(3) if 3 * g + b < GROUP)
PIECES = GROUP
HBM = pl.BlockSpec(memory_space=pltpu.HBM)


def iota(shape, dim):
    return lax.broadcasted_iota(jnp.int32, shape, dim)


def dot(a, b):
    return jnp.dot(a, b, preferred_element_type=F32)


def row_parts(k):
    inner = jnp.bitwise_and(k, BLOCK - 1)
    group = (
        (inner >= SLOTS).astype(jnp.int32)
        + (inner >= 2 * SLOTS).astype(jnp.int32)
        + (inner >= 3 * SLOTS).astype(jnp.int32)
    )
    slot = jnp.right_shift(k, 4) * SLOTS + inner - SLOTS * group
    return slot, group


def as_row(column):
    return jnp.transpose(jnp.broadcast_to(column, (column.shape[0], HD)))[0:1, :]


def stream_slots(ids, pass_local):
    rows, width = ids.shape
    stream = iota((PAD, width), 0)
    spread = jnp.zeros((PAD, width), F32)
    place = jnp.full((PAD, width), -1, jnp.int32)
    for r in range(rows):
        inside = (stream >= r * width) & (stream < (r + 1) * width)
        spread = jnp.where(inside, ids[r : r + 1, :].astype(F32), spread)
        place = jnp.where(inside, stream - r * width, place)
    hit = place == iota((PAD, width), 1)
    passage = jnp.sum(jnp.where(hit, spread, 0.0), axis=1, keepdims=True)
    real = iota((PAD, 1), 0) < rows * width
    owner = jnp.floor((passage + 0.5) * (1.0 / pass_local))
    local = jnp.where(real, passage - owner * pass_local, 0.0)
    owner = jnp.where(real, owner, -1.0)
    same = owner == as_row(owner)
    earlier = iota((PAD, PAD), 1) < iota((PAD, PAD), 0)
    position = jnp.sum(jnp.where(same & earlier, 1.0, 0.0), axis=1, keepdims=True)
    return jnp.where(real, owner * SLOTS + position, -1.0), local


def remote(src, dst, send, recv, device):
    return pltpu.make_async_remote_copy(
        src_ref=src, dst_ref=dst, send_sem=send, recv_sem=recv, device_id=device, device_id_type=MESH
    )


def outward(k, stores):
    odd = jnp.bitwise_and(k, 1)
    return stores // 2 + jnp.where(odd == 1, lax.div(k, 2), -lax.div(k, 2))


def exchange_copy(k, me, tp, stores, msg, recv, send_sem, recv_sem):
    to = lax.rem(me + outward(k, stores), stores)
    return remote(
        msg.at[pl.ds(pl.multiple_of(to * BLOCK, BLOCK), BLOCK)],
        recv.at[pl.ds(pl.multiple_of(me * BLOCK, BLOCK), BLOCK)],
        send_sem.at[k],
        recv_sem.at[k],
        (to, tp),
    )


def pack(stores, slot, wide_ref, msg_ref):
    rows = stores * BLOCK
    row_slot, row_group = row_parts(iota((rows, 1), 0))
    wanted = jnp.where(row_group < 3, row_slot, -2).astype(F32)
    pick = jnp.where(wanted == as_row(slot), 1.0, 0.0).astype(BF)
    message = dot(pick, wide_ref[:, 2 * WIDE : 3 * WIDE])
    message = jnp.where(row_group == 1, dot(pick, wide_ref[:, WIDE : 2 * WIDE]), message)
    message = jnp.where(row_group == 0, dot(pick, wide_ref[:, 0:WIDE]), message)
    msg_ref[...] = message.astype(BF)


def sort_slots(n_chunks, pass_local, recv_ref, lower_ref, sorted_ref):
    rows = recv_ref.shape[0]
    places = sorted_ref.shape[0]
    _, group = row_parts(iota((rows, 1), 0))
    passage = recv_ref[:, 2 * HD : 3 * HD].astype(F32)
    lane = iota((rows, HD), 1).astype(F32)
    member = jnp.where((group == 2) & (passage == lane), 1.0, 0.0)
    rank = dot(lower_ref[...], member.astype(BF))
    counts = jnp.sum(member, axis=0, keepdims=True)
    chunks = jnp.floor((counts + (CHUNK - 1)) * (1.0 / CHUNK))
    upto = jnp.where(iota((HD, HD), 0) <= iota((HD, HD), 1), 1.0, 0.0).astype(BF)
    ends = dot(jnp.broadcast_to(chunks, (8, HD)).astype(BF), upto)[0:1, :]
    firsts = ends - chunks
    place = jnp.sum(member * (rank + CHUNK * firsts), axis=1, keepdims=True)
    one = pltpu.roll(jnp.broadcast_to(place, (rows, HD)), rows - SLOTS, 0)
    two = pltpu.roll(jnp.broadcast_to(place, (rows, HD)), rows - 2 * SLOTS, 0)
    place = jnp.where(group == 0, two, jnp.where(group == 1, one, place))
    place = jnp.where(group < 3, place, -1.0)
    place_row = jnp.transpose(place)[0:1, :]
    _, group_row = row_parts(iota((1, rows), 1))
    target = iota((places, 1), 0).astype(F32)
    for g in range(3):
        pick = jnp.where(target == jnp.where(group_row == g, place_row, -2.0), 1.0, 0.0).astype(BF)
        sorted_ref[:, g * WIDE : (g + 1) * WIDE] = dot(pick, recv_ref[...]).astype(BF)
    return place, jnp.where(iota((1, HD), 1) < pass_local, ends, 1e9)


def attend_chunks(n_chunks, pass_local, limits, sorted_ref, kv_ref, result_ref):
    lanes = iota((CHUNK, HD), 1)
    head_lane = jnp.bitwise_and(lanes, GROUP - 1)
    across = (((1,), (1,)), ((), ()))
    down = (((0,), (0,)), ((), ()))

    def attend(c, carry):
        index = jnp.sum(jnp.where(limits <= c.astype(F32), 1.0, 0.0)).astype(jnp.int32)
        index = jnp.clip(index, 0, pass_local - 1)
        at = pl.ds(pl.multiple_of(c * CHUNK, CHUNK), CHUNK)
        queries = jnp.concatenate(
            [sorted_ref[at, h * HD : (h + 1) * HD] for h in range(GROUP)], axis=0
        )
        scores = lax.dot_general(kv_ref[0, index], queries, across, preferred_element_type=F32)
        highest = jnp.max(scores, axis=0, keepdims=True)
        terms = jnp.exp2((scores - highest) * (SCALE * 1.4426950408889634))
        total = jnp.sum(terms, axis=0, keepdims=True)
        mixed = lax.dot_general(
            kv_ref[1, index], terms.astype(BF), down, preferred_element_type=F32
        )
        mixed = jnp.transpose(mixed * (1.0 / total))
        lse = highest * SCALE + jnp.log(total)
        lse = jnp.transpose(jnp.broadcast_to(lse, (8, GROUP * CHUNK)))[:, 0:1]
        sums = jnp.zeros((CHUNK, HD), F32)
        for h in range(GROUP):
            part = slice(h * CHUNK, (h + 1) * CHUNK)
            result_ref[at, h * HD : (h + 1) * HD] = mixed[part].astype(BF)
            sums = jnp.where(head_lane == h, lse[part], sums)
        high = sums.astype(BF).astype(F32)
        middle = (sums - high).astype(BF).astype(F32)
        low = sums - high - middle
        sums = jnp.where(lanes < GROUP, high, jnp.where(lanes < 2 * GROUP, middle, low))
        result_ref[at, GROUP * HD :] = sums.astype(BF)
        return carry

    lax.fori_loop(0, n_chunks, attend, 0, unroll=28)


def unsort(home, group, tile, result_ref, back_ref):
    back = dot(home, result_ref[:, (6 + tile) * HD : (7 + tile) * HD])
    back = jnp.where(group == 1, dot(home, result_ref[:, (3 + tile) * HD : (4 + tile) * HD]), back)
    back = jnp.where(group == 0, dot(home, result_ref[:, tile * HD : (tile + 1) * HD]), back)
    back_ref[tile] = back.astype(BF)


def kernel(
    stores,
    tps,
    y_chips,
    pass_local,
    n_chunks,
    q_hbm,
    new_hbm,
    kv_hbm,
    id_hbm,
    res_hbm,
    w_hbm,
    out_ref,
    q_ref,
    new_ref,
    kv_ref,
    id_ref,
    res_ref,
    wide,
    msg,
    recv,
    lower,
    sorted_ref,
    result,
    back,
    home,
    block,
    weight,
    part,
    pair,
    both,
    others,
    total,
    final,
    load_sem,
    go_send,
    go_recv,
    ex_send,
    ex_recv,
    w_send,
    w_recv,
    right_send,
    right_recv,
    left_send,
    left_recv,
    pair_send,
    pair_recv,
    sum_send,
    sum_recv,
    end_send,
    end_recv,
):
    me, tp = lax.axis_index("store"), lax.axis_index("tp")
    zs = stores // y_chips
    z = lax.div(me, y_chips)
    y = me - z * y_chips
    streams, width = q_ref.shape
    w_cols = w_hbm.shape[1]
    cut = width // tps
    diagonal = z == tp
    barrier = pltpu.get_barrier_semaphore()

    def greet(device):
        pl.semaphore_signal(barrier, inc=1, device_id=device, device_id_type=MESH)

    def greet_store(k, carry):
        greet((lax.rem(me + outward(k, stores), stores), tp))
        return carry

    lax.fori_loop(1, stores, greet_store, 0)
    for k in range(1, tps):
        greet((me, lax.rem(tp + k, tps)))
    for other in range(tps):

        @pl.when(jnp.logical_not(diagonal & (tp == other)))
        def _():
            greet((tp * y_chips + y, other))

    loads = [
        pltpu.make_async_copy(src, dst, load_sem.at[i])
        for i, (src, dst) in enumerate(
            [
                (id_hbm, id_ref),
                (q_hbm, q_ref),
                (kv_hbm, kv_ref),
                (new_hbm, new_ref),
                (res_hbm, res_ref),
                (w_hbm, weight.at[y]),
            ]
        )
    ]
    for load in loads:
        load.start()

    loads[0].wait()
    slot, local = stream_slots(id_ref[...], pass_local)
    wide[streams:, 0:width] = jnp.zeros((PAD - streams, width), BF)
    wide[:, width:] = jnp.broadcast_to(local, (PAD, HD)).astype(BF)
    loads[1].wait()
    wide[0:streams, 0:width] = q_ref[...]
    pack(stores, slot, wide, msg)
    pl.semaphore_wait(barrier, stores + 2 * tps - 2 - diagonal.astype(jnp.int32))

    def go(k, carry):
        exchange_copy(k, me, tp, stores, msg, recv, go_send, go_recv).start()
        return carry

    def went(k, carry):
        exchange_copy(k, me, tp, stores, msg, recv, go_send, go_recv).wait()
        return carry

    lax.fori_loop(1, stores, go, 0)
    above = (z * y_chips + lax.rem(y + 1, y_chips), tp)
    below = (z * y_chips + lax.rem(y + y_chips - 1, y_chips), tp)
    middle = w_hbm.shape[0] // 2

    def weight_up(came):
        return remote(
            w_hbm,
            weight.at[lax.rem(y + y_chips - 1, y_chips) if came else y],
            w_send.at[0],
            w_recv.at[0],
            above,
        )

    def weight_down(came):
        return remote(
            w_hbm,
            weight.at[lax.rem(y + 1, y_chips) if came else y],
            w_send.at[1],
            w_recv.at[1],
            below,
        )

    def half_up(came):
        at = weight.at[lax.rem(y + y_chips - (2 if came else 1), y_chips), 0:middle]
        return remote(at, at, w_send.at[2], w_recv.at[2], above)

    def half_down(came):
        at = weight.at[lax.rem(y + (2 if came else 1), y_chips), middle:]
        return remote(at, at, w_send.at[3], w_recv.at[3], below)

    near = [weight_up, weight_down][: y_chips - 1]
    far = [half_up, half_down] if y_chips > 3 else []
    for copy in near:
        copy(False).start()

    mine = pl.ds(pl.multiple_of(me * BLOCK, BLOCK), BLOCK)
    recv[mine, :] = msg[mine, :]
    rows = stores * BLOCK
    lower[...] = jnp.where(iota((rows, rows), 1) < iota((rows, rows), 0), 1.0, 0.0).astype(BF)
    result[n_chunks * CHUNK :, :] = jnp.zeros(
        (result.shape[0] - n_chunks * CHUNK, result.shape[1]), BF
    )
    loads[3].wait()
    new_key = new_ref[0].astype(F32)
    new_value = new_ref[1].astype(F32)
    own = [
        jnp.sum(q_ref[:, h * HD : (h + 1) * HD].astype(F32) * new_key, axis=1, keepdims=True)
        * SCALE
        for h in range(GROUP)
    ]
    loads[2].wait()
    lax.fori_loop(1, stores, went, 0)

    place, limits = sort_slots(n_chunks, pass_local, recv, lower, sorted_ref)
    attend_chunks(n_chunks, pass_local, limits, sorted_ref, kv_ref, result)
    for copy in near:
        copy(True).wait_recv()
    for copy in far:
        copy(False).start()
    places = result.shape[0]
    spread = jnp.broadcast_to(place[:, 0:1], (rows, places))
    send_home = jnp.where(spread == iota((rows, places), 1).astype(F32), 1.0, 0.0).astype(BF)
    _, group = row_parts(iota((rows, 1), 0))

    def give(tile, k, carry):
        exchange_copy(
            k, me, tp, stores, back.at[tile], home.at[tile], ex_send.at[tile], ex_recv.at[tile]
        ).start()
        return carry

    def given(tile, k, carry):
        exchange_copy(
            k, me, tp, stores, back.at[tile], home.at[tile], ex_send.at[tile], ex_recv.at[tile]
        ).wait()
        return carry

    for tile in TILES:
        unsort(send_home, group, tile, result, back)
        lax.fori_loop(1, stores, functools.partial(give, tile), 0)
        home[tile, mine, :] = back[tile, mine, :]
    row_slot, row_group = row_parts(iota((1, rows), 1))
    match = slot[0:streams] == row_slot.astype(F32)
    picks = [jnp.where(match & (row_group == g), 1.0, 0.0).astype(BF) for g in range(3)]

    half = zs // 2
    to_right = (lax.rem(z + 1, zs) * y_chips + y, tp)
    to_left = (lax.rem(z + zs - 1, zs) * y_chips + y, tp)

    def on_right(k, c):
        return k < half or (k == half and c % 2 == 0)

    def on_left(k, c):
        return k < half or (k == half and c % 2 == 1)

    def right(k, c, came):
        at = block.at[lax.rem(z + zs - (k if came else k - 1), zs), c]
        return remote(at, at, right_send.at[k - 1, c], right_recv.at[k - 1, c], to_right)

    def left(k, c, came):
        at = block.at[lax.rem(z + (k if came else k - 1), zs), c]
        return remote(at, at, left_send.at[k - 1, c], left_recv.at[k - 1, c], to_left)

    def pass_on(k, c):
        if on_right(k, c):
            right(k, c, False).start()
        if on_left(k, c):
            left(k, c, False).start()

    for tile in TILES:
        lax.fori_loop(1, stores, functools.partial(given, tile), 0)
        if tile == 2:
            sums = dot(picks[2], home[tile])
        for h in range(tile, GROUP, 3):
            lse = sums[:, h : h + 1] + sums[:, GROUP + h : GROUP + h + 1]
            lse = lse + sums[:, 2 * GROUP + h : 2 * GROUP + h + 1]
            highest = jnp.maximum(lse, own[h])
            first = jnp.exp(lse - highest)
            second = jnp.exp(own[h] - highest)
            mixed = dot(picks[h // 3], home[tile]) * first + new_value * second
            piece = HEADS.index(h)
            block[z, piece] = (mixed * (1.0 / (first + second))).astype(BF)
            pass_on(1, piece)

    xs = tps // 2
    x = lax.div(tp, 2)
    core = tp - 2 * x

    def pair_copy(i):
        return remote(
            part.at[i, 1 - core], pair.at[i], pair_send.at[i], pair_recv.at[i], (me, 2 * x + 1 - core)
        )

    def sum_copy(i, k):
        to = lax.rem(x + k, xs)
        return remote(
            both.at[i, to], others.at[i, x], sum_send.at[i, k], sum_recv.at[i, k], (me, 2 * to + core)
        )

    def multiply(blocks):
        pieces = [
            jnp.concatenate([block[where[i], piece] for i in blocks], axis=0)
            for piece in range(PIECES)
        ]
        for v in range(y_chips):
            product = sum(
                dot(pieces[piece], weight[v, h * HD : (h + 1) * HD, :])
                for piece, h in enumerate(HEADS)
            )
            for n, i in enumerate(blocks):
                for u in range(w_cols // cut):
                    column = v * (w_cols // cut) + u
                    part[i, column % 2, column // 2] = product[
                        n * streams : (n + 1) * streams, u * cut : (u + 1) * cut
                    ].astype(BF)
        for i in blocks:
            pair_copy(i).start()

    def across(i):
        pair_copy(i).wait_recv()
        both[i] = (part[i, core].astype(F32) + pair[i].astype(F32)).astype(BF)
        for k in range(1, xs):
            sum_copy(i, k).start()

    def end_copy(i):
        return remote(
            total.at[i],
            final.at[tp],
            end_send.at[i],
            end_recv.at[tp],
            (where[i] * y_chips + y, z),
        )

    def add_up(i):
        value = part[i, core, x].astype(F32)
        for k in range(1, xs):
            sum_copy(i, k).wait_recv()
        value = value + pair[i, x].astype(F32)
        for k in range(1, xs):
            value = value + others[i, lax.rem(x + xs - k, xs)].astype(F32)
        total[i] = value.astype(BF)
        if i == 0:

            @pl.when(diagonal)
            def _():
                final[tp] = total[i]

            @pl.when(jnp.logical_not(diagonal))
            def _():
                end_copy(i).start()

        else:
            end_copy(i).start()

    offsets = [0]
    for k in range(1, half):
        offsets += [-k, k]
    offsets.append(-half)
    where = [lax.rem(z + zs + o, zs) for o in offsets]
    loads[5].wait()
    for copy in far:
        copy(True).wait_recv()
    ready = [[0]] + [[2 * k - 1, 2 * k] for k in range(1, half)] + [[zs - 1]]
    for k in range(1, half + 1):
        tasks = [functools.partial(multiply, ready[k - 1])]
        if k >= 2:
            tasks += [functools.partial(across, i) for i in ready[k - 2]]
        if k >= 3:
            tasks += [functools.partial(add_up, i) for i in ready[k - 3]]
        for c in range(PIECES):
            if on_right(k, c):
                right(k, c, True).wait_recv()
                if on_right(k + 1, c):
                    right(k + 1, c, False).start()
            if on_left(k, c):
                left(k, c, True).wait_recv()
                if on_left(k + 1, c):
                    left(k + 1, c, False).start()
            if c < len(tasks):
                tasks[c]()
    for i in ready[half - 1]:
        across(i)
    multiply(ready[half])
    for i in ready[half]:
        across(i)
    for blocks in ready[max(half - 2, 0) :]:
        for i in blocks:
            add_up(i)

    loads[4].wait()
    for other in range(tps):

        @pl.when(jnp.logical_not(diagonal & (tp == other)))
        def _():
            remote(
                total.at[0], final.at[other], end_send.at[0], end_recv.at[other], (me, tp)
            ).wait_recv()

        at = slice(other * cut, (other + 1) * cut)
        out_ref[:, at] = (res_ref[:, at].astype(F32) + final[other].astype(F32)).astype(BF)

    for copy in near + far:
        copy(False).wait_send()
    for k in range(1, half + 1):
        for c in range(PIECES):
            if on_right(k, c):
                right(k, c, False).wait_send()
            if on_left(k, c):
                left(k, c, False).wait_send()
    for i in range(zs):
        pair_copy(i).wait_send()
        for k in range(1, xs):
            sum_copy(i, k).wait_send()
        if i == 0:

            @pl.when(jnp.logical_not(diagonal))
            def _():
                end_copy(i).wait_send()

        else:
            end_copy(i).wait_send()


def shards(y_chips, query, new_kv, kv_store, passage_ids, residual_in, out_weight):
    stores, tps = lax.axis_size("store"), lax.axis_size("tp")
    zs = stores // y_chips
    streams, width = query.shape
    pass_local = kv_store.shape[1]
    rows = stores * BLOCK
    n_chunks = (stores * SLOTS + pass_local * (CHUNK - 1)) // CHUNK
    places = -(-n_chunks * CHUNK // HD) * HD
    cut = width // tps
    dma = pltpu.SemaphoreType.DMA

    def vmem(*shape):
        return pltpu.VMEM(shape, BF)

    return pl.pallas_call(
        functools.partial(kernel, stores, tps, y_chips, pass_local, n_chunks),
        out_shape=pltpu.VMEM((streams, width), BF),
        in_specs=[HBM] * 6,
        out_specs=VMEM,
        scratch_shapes=[
            vmem(streams, width),
            vmem(*new_kv.shape),
            vmem(*kv_store.shape),
            pltpu.VMEM(passage_ids.shape, jnp.int32),
            vmem(streams, width),
            vmem(PAD, 3 * WIDE),
            vmem(rows, WIDE),
            vmem(rows, WIDE),
            vmem(rows, rows),
            vmem(places, 3 * WIDE),
            vmem(places, 3 * WIDE),
            vmem(3, rows, HD),
            vmem(3, rows, HD),
            vmem(zs, PIECES, streams, width // PIECES),
            vmem(y_chips, *out_weight.shape),
            vmem(zs, 2, tps // 2, streams, cut),
            vmem(zs, tps // 2, streams, cut),
            vmem(zs, tps // 2, streams, cut),
            vmem(zs, tps // 2, streams, cut),
            vmem(zs, streams, cut),
            vmem(tps, streams, cut),
            dma((6,)),
            dma((stores,)),
            dma((stores,)),
            dma((3, stores)),
            dma((3, stores)),
            dma((4,)),
            dma((4,)),
            dma((zs // 2, PIECES)),
            dma((zs // 2, PIECES)),
            dma((zs // 2, PIECES)),
            dma((zs // 2, PIECES)),
            dma((zs,)),
            dma((zs,)),
            dma((zs, tps // 2)),
            dma((zs, tps // 2)),
            dma((zs,)),
            dma((tps,)),
        ],
        compiler_params=pltpu.CompilerParams(
            collective_id=0, has_side_effects=True, vmem_limit_bytes=48 * 2**20
        ),
        name="decode",
    )(*[pltpu.with_memory_space_constraint(a, pltpu.HBM) for a in (query, new_kv, kv_store, passage_ids, residual_in, out_weight)])


def solution(mesh, y_chips=Y_CHIPS):
    placed = (
        P("store", "tp"),
        P(None, "store", "tp"),
        P(None, "store", None, "tp"),
        P("store", None),
        P("store", "tp"),
        P("tp", "store"),
    )
    return jax.shard_map(
        functools.partial(shards, y_chips),
        mesh=mesh,
        in_specs=placed,
        out_specs=P("store", "tp"),
        check_vma=False,
    )
```
